32 devices in a mesh: row: 4 (over z), col: 8 (over y, x, core).
Axes of the slice: x: 2, y: 2, z: 4, core: 2. Of those that a mesh axis runs over, the one named last changes fastest.
Arguments:
- velocity_modes: bfloat16 [3, 2, 2, 2048, 1024], P(None, None, None, 'col', 'row'), may hold values from -6 to 6
- offsets: int32 [1024], P('row'), may hold values from 0 to 2047
- shear_steps: int32 [1], replicated, may hold values from 0 to 31
Outputs:
- advanced: bfloat16 [3, 2, 2, 2048, 1024], P(None, None, None, 'col', 'row')
The draws below stay inside these ranges and needn't reach their ends.
All inputs are finite; a program needn't handle non-finite values.
Results may differ from the reference program's by a relative error of at most 0.0085.
Values may be sent and summed in bfloat16 or wider, within the bound.
A program may use at most 128 MiB of HBM per device.

```python
import math
import jax
import jax.numpy as jnp
from jax import lax

NX = 2048
KX = 1024
NY = 2048
NZ = 2


def with_ends(entries, key, least, high):
    longest = entries.shape.index(max(entries.shape))
    spots = []
    for shift in (0, 1):
        where = [jax.random.randint(jax.random.fold_in(key, axis), (), 0, length) for axis, length in enumerate(entries.shape)]
        where[longest] = (where[longest] + shift) % entries.shape[longest]
        spots.append(tuple(where))
    return entries.at[spots[0]].set(least).at[spots[1]].set(high)


def block_levels(own_key, extent, pieces, low, high):
    def one(dim, parts):
        steps = jax.random.uniform(jax.random.fold_in(jax.random.fold_in(own_key, 6), dim), (parts,), jnp.float32, low / len(pieces), high / len(pieces))
        return jnp.repeat(jnp.exp(steps), extent[dim] // parts).reshape((-1,) + (1,) * (len(extent) - dim - 1))

    gain = one(*pieces[0])
    for cut in pieces[1:]:
        gain = gain * one(*cut)
    return gain


def scatter_about(own_key, shape, scale, most, pieces=(), kind=jnp.bfloat16):
    entries = scale * jax.random.normal(own_key, shape, jnp.float32)
    if pieces:
        entries = entries * block_levels(own_key, shape, pieces, -0.22, 0.18)
    return jnp.clip(entries, -most, most).astype(kind)


def setup_inputs(seed: int = 0) -> dict:
    arg_keys = jax.random.split(jax.random.key(seed), 4)
    velocity_modes = scatter_about(arg_keys[0], (3, 2, NZ, NY, KX), 1.0, 6.0, ((3, 8), (4, 4)))
    offsets = with_ends(jax.random.randint(arg_keys[1], (KX,), 0, NY), jax.random.fold_in(arg_keys[1], 1), 0, NY - 1).astype(jnp.int32)
    shear_steps = jax.random.randint(arg_keys[2], (1,), 0, 32).astype(jnp.int32)
    return dict(velocity_modes=velocity_modes, offsets=offsets, shear_steps=shear_steps)


dt_step = 0.1
period = 32.0
pair_table = ((0, 1, 2), (1, 3, 4), (2, 4, 5))
first_ids = (0, 0, 0, 1, 1, 2)
second_ids = (0, 1, 2, 1, 2, 2)

def round_real(values):
    narrow = values.astype(jnp.bfloat16)
    narrow = lax.optimization_barrier(narrow)
    return narrow.astype(jnp.float32)

def round_complex(values):
    return round_real(jnp.real(values)) + 1j * round_real(jnp.imag(values))

def advance(state_modes, modes, kx_ids, ky_ids, strain, x_count, y_count):
    ky_signed = (ky_ids + y_count // 2) % y_count - y_count // 2
    two_pi = 2.0 * math.pi
    kx_wave = two_pi * kx_ids.astype(jnp.float32) / x_count
    ky_wave = two_pi * ky_signed.astype(jnp.float32) / y_count - strain * kx_wave
    retain = ((3 * kx_ids < x_count) & (3 * jnp.abs(ky_signed) < y_count)).astype(jnp.float32)
    update = []
    for l in range(3):
        flux_real = kx_wave * modes[pair_table[l][0], 0].astype(jnp.float32) + ky_wave * modes[pair_table[l][1], 0].astype(jnp.float32)
        flux_imag = kx_wave * modes[pair_table[l][0], 1].astype(jnp.float32) + ky_wave * modes[pair_table[l][1], 1].astype(jnp.float32)
        update.append(jnp.stack([flux_imag, -flux_real]))
    update = jnp.stack(update)
    return (state_modes.astype(jnp.float32) + dt_step * retain * update).astype(jnp.bfloat16)

def reference(velocity_modes, offsets, shear_steps):
    spectrum = velocity_modes.astype(jnp.float32)
    row_index = (jnp.arange(NY, dtype=jnp.int32)[:, None] + offsets[None, :]) % NY
    remeshed = jnp.take_along_axis(spectrum, jnp.broadcast_to(row_index, spectrum.shape), axis=3)
    lines = remeshed[:, 0] + 1j * remeshed[:, 1]
    y_lines = round_complex(jnp.fft.ifft(lines, axis=2) * math.sqrt(NY))
    weights = jnp.where(jnp.arange(KX) == 0, 1.0, 2.0).astype(jnp.float32)
    padded = jnp.pad(y_lines * weights, ((0, 0), (0, 0), (0, 0), (0, NX - KX)))
    velocity = jnp.real(jnp.fft.ifft(padded, axis=3)) * math.sqrt(NX)

    def one_product(pair_ids):
        product = round_real(velocity[pair_ids[0]] * velocity[pair_ids[1]])
        x_modes = round_complex(jnp.fft.fft(product, axis=2)[:, :, :KX] / math.sqrt(NX))
        y_modes = round_complex(jnp.fft.fft(x_modes, axis=1) / math.sqrt(NY))
        return jnp.stack([jnp.real(y_modes), jnp.imag(y_modes)]).astype(jnp.float32)
    pair_list = jnp.stack([jnp.array(first_ids, dtype=jnp.int32), jnp.array(second_ids, dtype=jnp.int32)], 1)
    products = lax.map(one_product, pair_list)
    kx_ids = jnp.arange(KX, dtype=jnp.int32)[None, None, :]
    ky_ids = jnp.arange(NY, dtype=jnp.int32)[None, :, None]
    strain = shear_steps[0].astype(jnp.float32) / period - 0.5
    return advance(remeshed, products, kx_ids, ky_ids, strain, NX, NY)
```

```python
import functools
import math

import jax
import jax.numpy as jnp
import ml_dtypes
import numpy as np
from jax import lax
from jax.experimental import pallas as pl
from jax.experimental.pallas import tpu as pltpu
from jax.sharding import PartitionSpec as P

dt_step = 0.1
period = 32.0
pair_table = ((0, 1), (1, 3), (2, 4))
pairs = ((0, 0), (0, 1), (0, 2), (1, 1), (1, 2))
n_pairs = len(pairs)
bf16 = jnp.bfloat16
f32 = jnp.float32


def waves(rows, columns, length):
    angles = (2.0 * math.pi / length) * ((rows[:, None] * columns[None, :]) % length)
    scale = 1.0 / math.sqrt(length)
    return np.cos(angles) * scale, np.sin(angles) * scale


def narrow(matrix):
    return matrix.astype(ml_dtypes.bfloat16)


def y_table(length, columns):
    cosine, sine = waves(np.arange(length), columns, length)
    return narrow(np.concatenate([cosine, sine], 1))


def x_inverse_table(length, kb):
    ids = np.arange(length // 2)
    cosine, sine = waves(np.arange(length), ids, length)
    weight = np.where(ids == 0, 1.0, 2.0)
    both = np.stack([cosine * weight, -sine * weight], 1)
    both = both.reshape(length, 2, length // 2 // kb, kb).transpose(0, 2, 1, 3)
    return narrow(both.reshape(length, length))


def x_forward_table(length, kb, kept):
    cosine, sine = waves(np.arange(kept * kb), np.arange(length), length)
    both = np.stack([cosine, -sine]).reshape(2, kept, kb, length).transpose(1, 0, 2, 3)
    return narrow(both.reshape(kept * 2 * kb, length))


def exchange_kernel(rows, cols, wide, kept, cid, in_ref, out_ref, send_sem, recv_sem, own_sem):
    row, col = lax.axis_index("row"), lax.axis_index("col")
    count = rows * cols if wide else cols
    me = row * cols + col if wide else col

    def place(d):
        return (d // cols, d % cols) if wide else (row, d)

    barrier = pltpu.get_barrier_semaphore()

    def greet(s, c):
        other = (me + s) % count
        pl.semaphore_signal(
            barrier, inc=1, device_id=place(other), device_id_type=pl.DeviceIdType.MESH
        )
        return c

    lax.fori_loop(1, count, greet, 0)
    pl.semaphore_wait(barrier, count - 1)

    def copy(s):
        other = (me + s) % count
        source = (me + count - s) % count
        send = pltpu.make_async_remote_copy(
            src_ref=in_ref.at[jnp.minimum(other, kept - 1)],
            dst_ref=out_ref.at[me],
            send_sem=send_sem.at[s],
            recv_sem=recv_sem.at[s],
            device_id=place(other),
            device_id_type=pl.DeviceIdType.MESH,
        )
        return other, source, send

    own = pltpu.make_async_copy(in_ref.at[jnp.minimum(me, kept - 1)], out_ref.at[me], own_sem)

    def begin(s, c):
        other, _, send = copy(s)

        @pl.when(other < kept)
        def _():
            send.start()

        return c

    lax.fori_loop(1, count, begin, 0)
    own.start()
    own.wait()

    def finish(s, c):
        other, _, send = copy(s)

        @pl.when(other < kept)
        def _():
            send.wait_send()

        @pl.when(me < kept)
        def _():
            send.wait_recv()

        return c

    lax.fori_loop(1, count, finish, 0)


def exchange(blocks, rows, cols, wide, cid):
    count = rows * cols if wide else cols
    kept = blocks.shape[0]
    return pl.pallas_call(
        functools.partial(exchange_kernel, rows, cols, wide, kept, cid),
        out_shape=jax.ShapeDtypeStruct((count,) + blocks.shape[1:], blocks.dtype),
        in_specs=[pl.BlockSpec(memory_space=pl.ANY)],
        out_specs=pl.BlockSpec(memory_space=pl.ANY),
        scratch_shapes=[
            pltpu.SemaphoreType.DMA((count,)),
            pltpu.SemaphoreType.DMA((count,)),
            pltpu.SemaphoreType.DMA,
        ],
        compiler_params=pltpu.CompilerParams(collective_id=cid, has_side_effects=True),
    )(blocks)


def roll_kernel(length, offs_ref, in_ref, out_ref):
    value = jnp.concatenate(
        [in_ref[s, 0].astype(f32) for s in range(in_ref.shape[0])], axis=1
    )
    offs = offs_ref[...]
    stride = 1
    while stride < length:
        chosen = (offs // stride) % 2 == 1
        value = jnp.where(chosen, pltpu.roll(value, length - stride, 1), value)
        stride *= 2
    out_ref[0] = value.astype(out_ref.dtype)


def remesh(blocks, offs):
    sources, groups, kb, yl = blocks.shape
    length = sources * yl
    return pl.pallas_call(
        functools.partial(roll_kernel, length),
        grid=(groups,),
        out_shape=jax.ShapeDtypeStruct((groups, kb, length), blocks.dtype),
        in_specs=[
            pl.BlockSpec((kb, 1), lambda i: (0, 0)),
            pl.BlockSpec((sources, 1, kb, yl), lambda i: (0, i, 0, 0)),
        ],
        out_specs=pl.BlockSpec((1, kb, length), lambda i: (i, 0, 0)),
    )(offs.reshape(kb, 1), blocks)


def dot(a, b):
    return jnp.dot(a, b, preferred_element_type=f32)


def local(velocity_modes, offsets, shear_steps):
    nz, yl, kl = velocity_modes.shape[2:]
    rows, cols = lax.axis_size("row"), lax.axis_size("col")
    devices = rows * cols
    ny, nk = yl * cols, kl * rows
    nx = 2 * nk
    kb = kl // cols
    gb = ny * nz // devices
    gn = ny // gb
    row, col = lax.axis_index("row"), lax.axis_index("col")
    strain = shear_steps[0].astype(f32) / period - 0.5

    parts = velocity_modes.reshape(6 * nz, yl, cols, kb).transpose(2, 0, 3, 1)
    parts = exchange(parts, rows, cols, False, 1)
    offs = lax.dynamic_slice(offsets, (col * kb,), (kb,))
    remeshed = remesh(parts, offs)

    every = np.arange(ny)
    both = dot(remeshed.reshape(-1, ny), jnp.asarray(y_table(ny, every)))
    both = both.reshape(3, 2, nz, kb, 2, ny)
    real = both[:, 0, :, :, 0] - both[:, 1, :, :, 1]
    imag = both[:, 0, :, :, 1] + both[:, 1, :, :, 0]
    lines = jnp.stack([real, imag]).astype(bf16).reshape(2, 3, nz, kb, gn, gb)
    lines = lines.transpose(2, 4, 0, 3, 1, 5).reshape(devices, 2 * kb, 3 * gb)
    lines = exchange(lines, rows, cols, True, 2).reshape(2 * nk, 3 * gb)

    velocity = dot(jnp.asarray(x_inverse_table(nx, kb)), lines)
    v = [velocity[:, c * gb : (c + 1) * gb] for c in range(3)]
    products = jnp.concatenate([(v[a] * v[b]).astype(bf16) for a, b in pairs], 1)
    kept = -(-(-(-nx // 3)) // kb)
    x_modes = dot(jnp.asarray(x_forward_table(nx, kb, kept)), products).astype(bf16)
    x_modes = x_modes.reshape(kept, 2 * kb, n_pairs * gb)
    x_modes = exchange(x_modes, rows, cols, True, 3)

    x_modes = x_modes.reshape(nz, gn, 2, kb, n_pairs, gb).transpose(4, 2, 0, 3, 1, 5)
    low = -(-(-(-ny // 3)) // 128) * 128
    near = np.concatenate([np.arange(low), np.arange(ny - low, ny)])
    both = dot(x_modes.reshape(-1, ny), jnp.asarray(y_table(ny, near)))
    both = both.reshape(n_pairs, 2, nz, kb, 2, 2 * low)
    real = both[:, 0, :, :, 0] + both[:, 1, :, :, 1]
    imag = both[:, 1, :, :, 0] - both[:, 0, :, :, 1]

    kx = ((row * cols + col) * kb + jnp.arange(kb, dtype=jnp.int32))[:, None]
    ys = jnp.concatenate(
        [jnp.arange(low, dtype=jnp.int32), jnp.arange(-low, 0, dtype=jnp.int32)]
    )[None, :]
    k1 = 2.0 * math.pi * kx.astype(f32) / nx
    k2 = 2.0 * math.pi * ys.astype(f32) / ny - strain * k1
    retain = (3 * kx < nx) & (3 * jnp.abs(ys) < ny)
    update = []
    for l in range(3):
        e0, e1 = pair_table[l]
        flux_real = k1 * real[e0] + k2 * real[e1]
        flux_imag = k1 * imag[e0] + k2 * imag[e1]
        update.append(jnp.stack([flux_imag, -flux_real]))
    update = jnp.where(retain, dt_step * jnp.stack(update), 0.0)
    state = remeshed.reshape(3, 2, nz, kb, ny)
    advanced = jnp.concatenate(
        [
            (state[..., :low].astype(f32) + update[..., :low]).astype(bf16),
            state[..., low : ny - low],
            (state[..., ny - low :].astype(f32) + update[..., low:]).astype(bf16),
        ],
        -1,
    )
    parts = advanced.reshape(6 * nz, kb, cols, yl).transpose(2, 0, 1, 3)
    parts = exchange(parts, rows, cols, False, 4)
    out = parts.transpose(1, 3, 0, 2)
    return out.reshape(3, 2, nz, yl, kl)


def solution(mesh):
    return jax.shard_map(
        local,
        mesh=mesh,
        in_specs=(P(None, None, None, "col", "row"), P("row"), P()),
        out_specs=P(None, None, None, "col", "row"),
        check_vma=False,
    )
```

```python
import functools
import math

import jax
import jax.numpy as jnp
import ml_dtypes
import numpy as np
from jax import lax
from jax.experimental import pallas as pl
from jax.experimental.pallas import tpu as pltpu
from jax.sharding import PartitionSpec as P

dt_step = 0.1
period = 32.0
pair_table = ((0, 1), (1, 3), (2, 4))
pairs = ((0, 0), (0, 1), (0, 2), (1, 1), (1, 2))
n_pairs = len(pairs)
bf16 = jnp.bfloat16
f32 = jnp.float32


def waves(rows, columns, length):
    angles = (2.0 * math.pi / length) * ((rows[:, None] * columns[None, :]) % length)
    scale = 1.0 / math.sqrt(length)
    return np.cos(angles) * scale, np.sin(angles) * scale


def narrow(matrix):
    return matrix.astype(ml_dtypes.bfloat16)


def y_table(length, columns):
    cosine, sine = waves(np.arange(length), columns, length)
    return narrow(np.concatenate([cosine, sine], 1))


def x_inverse_table(length, kb):
    ids = np.arange(length // 2)
    cosine, sine = waves(np.arange(length), ids, length)
    weight = np.where(ids == 0, 1.0, 2.0)
    both = np.stack([cosine * weight, -sine * weight], 1)
    both = both.reshape(length, 2, length // 2 // kb, kb).transpose(0, 2, 1, 3)
    return narrow(both.reshape(length, length))


def x_forward_table(length, kb, kept):
    cosine, sine = waves(np.arange(kept * kb), np.arange(length), length)
    both = np.stack([cosine, -sine]).reshape(2, kept, kb, length).transpose(1, 0, 2, 3)
    return narrow(both.reshape(kept * 2 * kb, length))


def exchange_kernel(rows, cols, wide, kept, cid, in_ref, out_ref, send_sem, recv_sem, own_sem):
    row, col = lax.axis_index("row"), lax.axis_index("col")
    count = rows * cols if wide else cols
    me = row * cols + col if wide else col

    def place(d):
        return (d // cols, d % cols) if wide else (row, d)

    barrier = pltpu.get_barrier_semaphore()

    def greet(s, c):
        other = (me + s) % count
        pl.semaphore_signal(
            barrier, inc=1, device_id=place(other), device_id_type=pl.DeviceIdType.MESH
        )
        return c

    lax.fori_loop(1, count, greet, 0)
    pl.semaphore_wait(barrier, count - 1)

    def copy(s):
        other = (me + s) % count
        source = (me + count - s) % count
        send = pltpu.make_async_remote_copy(
            src_ref=in_ref.at[jnp.minimum(other, kept - 1)],
            dst_ref=out_ref.at[me],
            send_sem=send_sem.at[s],
            recv_sem=recv_sem.at[s],
            device_id=place(other),
            device_id_type=pl.DeviceIdType.MESH,
        )
        return other, source, send

    own = pltpu.make_async_copy(in_ref.at[jnp.minimum(me, kept - 1)], out_ref.at[me], own_sem)

    def begin(s, c):
        other, _, send = copy(s)

        @pl.when(other < kept)
        def _():
            send.start()

        return c

    lax.fori_loop(1, count, begin, 0)
    own.start()
    own.wait()

    def finish(s, c):
        other, _, send = copy(s)

        @pl.when(other < kept)
        def _():
            send.wait_send()

        @pl.when(me < kept)
        def _():
            send.wait_recv()

        return c

    lax.fori_loop(1, count, finish, 0)


def exchange(blocks, rows, cols, wide, cid):
    count = rows * cols if wide else cols
    kept = blocks.shape[0]
    return pl.pallas_call(
        functools.partial(exchange_kernel, rows, cols, wide, kept, cid),
        out_shape=jax.ShapeDtypeStruct((count,) + blocks.shape[1:], blocks.dtype),
        in_specs=[pl.BlockSpec(memory_space=pl.ANY)],
        out_specs=pl.BlockSpec(memory_space=pl.ANY),
        scratch_shapes=[
            pltpu.SemaphoreType.DMA((count,)),
            pltpu.SemaphoreType.DMA((count,)),
            pltpu.SemaphoreType.DMA,
        ],
        compiler_params=pltpu.CompilerParams(collective_id=cid, has_side_effects=True),
    )(blocks)


def roll_kernel(length, offs_ref, in_ref, out_ref):
    value = jnp.concatenate(
        [in_ref[s, 0].astype(f32) for s in range(in_ref.shape[0])], axis=1
    )
    offs = offs_ref[...]
    stride = 1
    while stride < length:
        chosen = (offs // stride) % 2 == 1
        value = jnp.where(chosen, pltpu.roll(value, length - stride, 1), value)
        stride *= 2
    out_ref[0] = value.astype(out_ref.dtype)


def remesh(blocks, offs):
    sources, groups, kb, yl = blocks.shape
    length = sources * yl
    return pl.pallas_call(
        functools.partial(roll_kernel, length),
        grid=(groups,),
        out_shape=jax.ShapeDtypeStruct((groups, kb, length), blocks.dtype),
        in_specs=[
            pl.BlockSpec((kb, 1), lambda i: (0, 0)),
            pl.BlockSpec((sources, 1, kb, yl), lambda i: (0, i, 0, 0)),
        ],
        out_specs=pl.BlockSpec((1, kb, length), lambda i: (i, 0, 0)),
    )(offs.reshape(kb, 1), blocks)


def dot(a, b):
    return jnp.dot(a, b, preferred_element_type=f32)


def greet_all(count, me, place):
    barrier = pltpu.get_barrier_semaphore()

    def greet(s, c):
        pl.semaphore_signal(
            barrier,
            inc=1,
            device_id=place((me + s) % count),
            device_id_type=pl.DeviceIdType.MESH,
        )
        return c

    lax.fori_loop(1, count, greet, 0)
    return lambda: pl.semaphore_wait(barrier, count - 1)


def back_kernel(
    rows, cols, nx, ny, nz,
    modes_ref, state_ref, strain_ref, table_ref, out_ref,
    table, lines, block, table_sem, send_sem, recv_sem, own_sem,
):
    row, col = lax.axis_index("row"), lax.axis_index("col")
    groups, kb, _ = state_ref.shape
    yl = ny // cols
    half = table_ref.shape[0] // 2
    gn = modes_ref.shape[0] // nz
    gb = modes_ref.shape[2] // n_pairs
    first_k = (row * cols + col) * kb
    wait_all = greet_all(cols, col, lambda d: (row, d))
    live = 3 * first_k < nx

    def fetch(i):
        return pltpu.make_async_copy(table_ref.at[i], table.at[i], table_sem.at[i])

    for i in range(2 * half):
        fetch(i).start()
    for e in range(n_pairs):
        for p in range(2):
            for z in range(nz):
                top = ((e * 2 + p) * nz + z) * kb
                for b in range(gn):
                    lines[top : top + kb, b * gb : (b + 1) * gb] = modes_ref[
                        z * gn + b, p * kb : (p + 1) * kb, e * gb : (e + 1) * gb
                    ]
    for i in range(2 * half):
        fetch(i).wait()
    wait_all()

    def send(s):
        other = (col + s) % cols
        return pltpu.make_async_remote_copy(
            src_ref=block.at[other],
            dst_ref=out_ref.at[col],
            send_sem=send_sem.at[s],
            recv_sem=recv_sem.at[s],
            device_id=(row, other),
            device_id_type=pl.DeviceIdType.MESH,
        )

    def make(j):
        kept = live & ((j < half) | (j >= cols - half))
        columns = pl.ds(pl.multiple_of(j * yl, yl), yl)

        @pl.when(kept)
        def _():
            i = jnp.where(j < half, j, j - (cols - 2 * half))
            both = dot(lines[...], table[i])
            kx = first_k + lax.broadcasted_iota(jnp.int32, (kb, yl), 0)
            ky = j * yl + lax.broadcasted_iota(jnp.int32, (kb, yl), 1)
            ys = jnp.where(ky < ny // 2, ky, ky - ny)
            k1 = (2.0 * math.pi / nx) * kx.astype(f32)
            k2 = (2.0 * math.pi / ny) * ys.astype(f32) - strain_ref[...] * k1
            retain = (3 * kx < nx) & (3 * jnp.abs(ys) < ny)

            def mode(e, z):
                a = both[((e * 2) * nz + z) * kb : ((e * 2) * nz + z + 1) * kb]
                b = both[((e * 2 + 1) * nz + z) * kb : ((e * 2 + 1) * nz + z + 1) * kb]
                return a[:, :yl] + b[:, yl:], b[:, :yl] - a[:, yl:]

            for z in range(nz):
                found = [mode(e, z) for e in range(n_pairs)]
                for l in range(3):
                    e0, e1 = pair_table[l]
                    flux_real = k1 * found[e0][0] + k2 * found[e1][0]
                    flux_imag = k1 * found[e0][1] + k2 * found[e1][1]
                    for p, update in ((0, flux_imag), (1, -flux_real)):
                        g = (l * 2 + p) * nz + z
                        state = state_ref[g, :, columns].astype(f32)
                        change = jnp.where(retain, dt_step * update, 0.0)
                        block[j, g] = (state + change).astype(bf16)

        @pl.when(jnp.logical_not(kept))
        def _():
            for g in range(groups):
                block[j, g] = state_ref[g, :, columns]

    def step(s, c):
        make((col + s) % cols)
        send(s).start()
        return c

    lax.fori_loop(1, cols, step, 0)
    make(col)
    own = pltpu.make_async_copy(block.at[col], out_ref.at[col], own_sem)
    own.start()
    own.wait()

    def finish(s, c):
        send(s).wait()
        return c

    lax.fori_loop(1, cols, finish, 0)


def back(modes, state, strain, rows, cols, nx, ny, nz):
    groups, kb, _ = state.shape
    yl = ny // cols
    half = -(-(-(-ny // 3)) // yl)
    cosine, sine = waves(np.arange(ny), np.arange(ny), ny)
    kept = [j for j in range(cols) if j < half or j >= cols - half]
    table = np.stack(
        [
            np.concatenate([m[:, j * yl : (j + 1) * yl] for m in (cosine, sine)], 1)
            for j in kept
        ]
    )
    whole = pl.BlockSpec(memory_space=pltpu.VMEM)
    far = pl.BlockSpec(memory_space=pl.ANY)
    return pl.pallas_call(
        functools.partial(back_kernel, rows, cols, nx, ny, nz),
        out_shape=jax.ShapeDtypeStruct((cols, groups, kb, yl), bf16),
        in_specs=[whole, whole, whole, far],
        out_specs=far,
        scratch_shapes=[
            pltpu.VMEM(table.shape, bf16),
            pltpu.VMEM((n_pairs * 2 * nz * kb, ny), bf16),
            pltpu.VMEM((cols, groups, kb, yl), bf16),
            pltpu.SemaphoreType.DMA((len(kept),)),
            pltpu.SemaphoreType.DMA((cols,)),
            pltpu.SemaphoreType.DMA((cols,)),
            pltpu.SemaphoreType.DMA,
        ],
        compiler_params=pltpu.CompilerParams(
            collective_id=5, has_side_effects=True, vmem_limit_bytes=44 * 2**20
        ),
    )(modes, state, strain.reshape(1, 1), jnp.asarray(narrow(table)))


def ahead_kernel(
    rows, cols, ny, nz,
    in_ref, offs_ref, table_ref, lines_ref, state_ref,
    table, came, state, block,
    table_sem, send_sem, recv_sem, own_sem, far_send, far_recv, far_own,
):
    row, col = lax.axis_index("row"), lax.axis_index("col")
    count = rows * cols
    me = row * cols + col
    groups, kb, yl = in_ref.shape[1:]
    gb = lines_ref.shape[2] // 3
    gn = count // nz
    tiles, _, wide = table_ref.shape
    width = wide // 2
    per = width // gb

    def place(d):
        return (d // cols, d % cols)

    wait_all = greet_all(count, me, place)

    def fetch(i):
        return pltpu.make_async_copy(table_ref.at[i], table.at[i], table_sem.at[i])

    def near(s):
        other = (col + s) % cols
        return pltpu.make_async_remote_copy(
            src_ref=in_ref.at[other],
            dst_ref=came.at[col],
            send_sem=send_sem.at[s],
            recv_sem=recv_sem.at[s],
            device_id=(row, other),
            device_id_type=pl.DeviceIdType.MESH,
        )

    wait_all()
    for s in range(1, cols):
        near(s).start()
    own = pltpu.make_async_copy(in_ref.at[col], came.at[col], own_sem)
    own.start()
    for i in range(tiles):
        fetch(i).start()
    for i in range(tiles):
        fetch(i).wait()
    own.wait()
    for s in range(1, cols):
        near(s).wait()

    def gather(g, c):
        top = pl.multiple_of(g * kb, kb)
        for s in range(cols):
            state[pl.ds(top, kb), s * yl : (s + 1) * yl] = came[s, g]
        return c

    lax.fori_loop(0, groups, gather, 0)

    def far(s):
        other = (me + s) % count
        return pltpu.make_async_remote_copy(
            src_ref=block.at[other],
            dst_ref=lines_ref.at[me],
            send_sem=far_send.at[s],
            recv_sem=far_recv.at[s],
            device_id=place(other),
            device_id_type=pl.DeviceIdType.MESH,
        )

    offs = offs_ref[...]

    def tile(step, c):
        t = (me // nz + step) % tiles
        both = dot(state[...], table[t])
        gy = t * width + lax.broadcasted_iota(jnp.int32, (kb, width), 1)
        turn = (offs * gy) % ny
        turn = jnp.where(turn < ny // 2, turn, turn - ny)
        angle = (2.0 * math.pi / ny) * turn.astype(f32)
        cosine, sine = jnp.cos(angle), jnp.sin(angle)
        for c in range(3):
            for z in range(nz):
                a = both[((c * 2) * nz + z) * kb : ((c * 2) * nz + z + 1) * kb]
                b = both[((c * 2 + 1) * nz + z) * kb : ((c * 2 + 1) * nz + z + 1) * kb]
                real = a[:, :width] - b[:, width:]
                imag = a[:, width:] + b[:, :width]
                turned = (cosine * real + sine * imag, cosine * imag - sine * real)
                for h in range(per):
                    d = z * gn + t * per + h
                    for p in range(2):
                        block[d, p * kb : (p + 1) * kb, c * gb : (c + 1) * gb] = turned[p][
                            :, h * gb : (h + 1) * gb
                        ].astype(bf16)
        for z in range(nz):
            for h in range(per):
                d = z * gn + t * per + h

                @pl.when(d != me)
                def _():
                    far((d - me + count) % count).start()

        return 0

    lax.fori_loop(0, tiles, tile, 0)
    far_copy = pltpu.make_async_copy(block.at[me], lines_ref.at[me], far_own)
    far_copy.start()

    def shift(g, c):
        top = pl.multiple_of(g * kb, kb)
        value = state[pl.ds(top, kb), :].astype(f32)
        stride = 1
        while stride < ny:
            chosen = (offs // stride) % 2 == 1
            value = jnp.where(chosen, pltpu.roll(value, ny - stride, 1), value)
            stride *= 2
        state_ref[g] = value.astype(bf16)
        return c

    lax.fori_loop(0, groups, shift, 0)
    far_copy.wait()

    def finish(s, c):
        far(s).wait()
        return c

    lax.fori_loop(1, count, finish, 0)


def ahead(parts, offs, rows, cols, ny, nz, gb):
    groups, kb, yl = parts.shape[1:]
    width = 2 * gb
    cosine, sine = waves(np.arange(ny), np.arange(ny), ny)
    table = np.stack(
        [
            np.concatenate([m[:, t : t + width] for m in (cosine, sine)], 1)
            for t in range(0, ny, width)
        ]
    )
    count = rows * cols
    whole = pl.BlockSpec(memory_space=pltpu.VMEM)
    far = pl.BlockSpec(memory_space=pl.ANY)
    dma = pltpu.SemaphoreType.DMA
    return pl.pallas_call(
        functools.partial(ahead_kernel, rows, cols, ny, nz),
        out_shape=(
            jax.ShapeDtypeStruct((count, 2 * kb, 3 * gb), bf16),
            jax.ShapeDtypeStruct((groups, kb, ny), bf16),
        ),
        in_specs=[far, whole, far],
        out_specs=(far, whole),
        scratch_shapes=[
            pltpu.VMEM(table.shape, bf16),
            pltpu.VMEM((cols, groups, kb, yl), bf16),
            pltpu.VMEM((groups * kb, ny), bf16),
            pltpu.VMEM((count, 2 * kb, 3 * gb), bf16),
            dma((table.shape[0],)),
            dma((cols,)),
            dma((cols,)),
            dma,
            dma((count,)),
            dma((count,)),
            dma,
        ],
        compiler_params=pltpu.CompilerParams(
            collective_id=6, has_side_effects=True, vmem_limit_bytes=44 * 2**20
        ),
    )(parts, offs.reshape(kb, 1), jnp.asarray(narrow(table)))


def local(velocity_modes, offsets, shear_steps):
    nz, yl, kl = velocity_modes.shape[2:]
    rows, cols = lax.axis_size("row"), lax.axis_size("col")
    devices = rows * cols
    ny, nk = yl * cols, kl * rows
    nx = 2 * nk
    kb = kl // cols
    gb = ny * nz // devices
    gn = ny // gb
    row, col = lax.axis_index("row"), lax.axis_index("col")
    strain = shear_steps[0].astype(f32) / period - 0.5

    parts = velocity_modes.reshape(6 * nz, yl, cols, kb).transpose(2, 0, 3, 1)
    offs = lax.dynamic_slice(offsets, (col * kb,), (kb,))
    aligned = kb % 16 == 0 and gb % 128 == 0 and yl % 128 == 0
    if aligned:
        lines, remeshed = ahead(parts, offs, rows, cols, ny, nz, gb)
    else:
        parts = exchange(parts, rows, cols, False, 1)
        remeshed = remesh(parts, offs)

        every = np.arange(ny)
        both = dot(remeshed.reshape(-1, ny), jnp.asarray(y_table(ny, every)))
        both = both.reshape(3, 2, nz, kb, 2, ny)
        real = both[:, 0, :, :, 0] - both[:, 1, :, :, 1]
        imag = both[:, 0, :, :, 1] + both[:, 1, :, :, 0]
        lines = jnp.stack([real, imag]).astype(bf16).reshape(2, 3, nz, kb, gn, gb)
        lines = lines.transpose(2, 4, 0, 3, 1, 5).reshape(devices, 2 * kb, 3 * gb)
        lines = exchange(lines, rows, cols, True, 2)
    lines = lines.reshape(2 * nk, 3 * gb)

    velocity = dot(jnp.asarray(x_inverse_table(nx, kb)), lines)
    v = [velocity[:, c * gb : (c + 1) * gb] for c in range(3)]
    products = jnp.concatenate([(v[a] * v[b]).astype(bf16) for a, b in pairs], 1)
    kept = -(-(-(-nx // 3)) // kb)
    x_modes = dot(jnp.asarray(x_forward_table(nx, kb, kept)), products).astype(bf16)
    x_modes = x_modes.reshape(kept, 2 * kb, n_pairs * gb)
    x_modes = exchange(x_modes, rows, cols, True, 3)

    if aligned:
        parts = back(x_modes, remeshed, strain, rows, cols, nx, ny, nz)
    else:
        x_modes = x_modes.reshape(nz, gn, 2, kb, n_pairs, gb).transpose(4, 2, 0, 3, 1, 5)
        low = -(-(-(-ny // 3)) // 128) * 128
        near = np.concatenate([np.arange(low), np.arange(ny - low, ny)])
        both = dot(x_modes.reshape(-1, ny), jnp.asarray(y_table(ny, near)))
        both = both.reshape(n_pairs, 2, nz, kb, 2, 2 * low)
        real = both[:, 0, :, :, 0] + both[:, 1, :, :, 1]
        imag = both[:, 1, :, :, 0] - both[:, 0, :, :, 1]

        kx = ((row * cols + col) * kb + jnp.arange(kb, dtype=jnp.int32))[:, None]
        ys = jnp.concatenate(
            [jnp.arange(low, dtype=jnp.int32), jnp.arange(-low, 0, dtype=jnp.int32)]
        )[None, :]
        k1 = 2.0 * math.pi * kx.astype(f32) / nx
        k2 = 2.0 * math.pi * ys.astype(f32) / ny - strain * k1
        retain = (3 * kx < nx) & (3 * jnp.abs(ys) < ny)
        update = []
        for l in range(3):
            e0, e1 = pair_table[l]
            flux_real = k1 * real[e0] + k2 * real[e1]
            flux_imag = k1 * imag[e0] + k2 * imag[e1]
            update.append(jnp.stack([flux_imag, -flux_real]))
        update = jnp.where(retain, dt_step * jnp.stack(update), 0.0)
        state = remeshed.reshape(3, 2, nz, kb, ny)
        advanced = jnp.concatenate(
            [
                (state[..., :low].astype(f32) + update[..., :low]).astype(bf16),
                state[..., low : ny - low],
                (state[..., ny - low :].astype(f32) + update[..., low:]).astype(bf16),
            ],
            -1,
        )
        parts = advanced.reshape(6 * nz, kb, cols, yl).transpose(2, 0, 1, 3)
        parts = exchange(parts, rows, cols, False, 4)
    out = parts.transpose(1, 3, 0, 2)
    return out.reshape(3, 2, nz, yl, kl)


def solution(mesh):
    return jax.shard_map(
        local,
        mesh=mesh,
        in_specs=(P(None, None, None, "col", "row"), P("row"), P()),
        out_specs=P(None, None, None, "col", "row"),
        check_vma=False,
    )
```

```python
import functools
import math

import jax
import jax.numpy as jnp
import ml_dtypes
import numpy as np
from jax import lax
from jax.experimental import pallas as pl
from jax.experimental.pallas import tpu as pltpu
from jax.sharding import PartitionSpec as P

dt_step = 0.1
period = 32.0
pair_table = ((0, 1), (1, 3), (2, 4))
pairs = ((0, 0), (0, 1), (0, 2), (1, 1), (1, 2))
n_pairs = len(pairs)
bf16 = jnp.bfloat16
f32 = jnp.float32


def waves(rows, columns, length):
    angles = (2.0 * math.pi / length) * ((rows[:, None] * columns[None, :]) % length)
    scale = 1.0 / math.sqrt(length)
    return np.cos(angles) * scale, np.sin(angles) * scale


def narrow(matrix):
    return matrix.astype(ml_dtypes.bfloat16)


def y_table(length, columns):
    cosine, sine = waves(np.arange(length), columns, length)
    return narrow(np.concatenate([cosine, sine], 1))


def x_inverse_table(length, kb):
    ids = np.arange(length // 2)
    cosine, sine = waves(np.arange(length), ids, length)
    weight = np.where(ids == 0, 1.0, 2.0)
    both = np.stack([cosine * weight, -sine * weight], 1)
    both = both.reshape(length, 2, length // 2 // kb, kb).transpose(0, 2, 1, 3)
    return narrow(both.reshape(length, length))


def x_forward_table(length, kb, kept):
    cosine, sine = waves(np.arange(kept * kb), np.arange(length), length)
    both = np.stack([cosine, -sine]).reshape(2, kept, kb, length).transpose(1, 0, 2, 3)
    return narrow(both.reshape(kept * 2 * kb, length))


def exchange_kernel(rows, cols, wide, kept, cid, in_ref, out_ref, send_sem, recv_sem, own_sem):
    row, col = lax.axis_index("row"), lax.axis_index("col")
    count = rows * cols if wide else cols
    me = row * cols + col if wide else col

    def place(d):
        return (d // cols, d % cols) if wide else (row, d)

    barrier = pltpu.get_barrier_semaphore()

    def greet(s, c):
        other = (me + s) % count
        pl.semaphore_signal(
            barrier, inc=1, device_id=place(other), device_id_type=pl.DeviceIdType.MESH
        )
        return c

    lax.fori_loop(1, count, greet, 0)
    pl.semaphore_wait(barrier, count - 1)

    def copy(s):
        other = (me + s) % count
        source = (me + count - s) % count
        send = pltpu.make_async_remote_copy(
            src_ref=in_ref.at[jnp.minimum(other, kept - 1)],
            dst_ref=out_ref.at[me],
            send_sem=send_sem.at[s],
            recv_sem=recv_sem.at[s],
            device_id=place(other),
            device_id_type=pl.DeviceIdType.MESH,
        )
        return other, source, send

    own = pltpu.make_async_copy(in_ref.at[jnp.minimum(me, kept - 1)], out_ref.at[me], own_sem)

    def begin(s, c):
        other, _, send = copy(s)

        @pl.when(other < kept)
        def _():
            send.start()

        return c

    lax.fori_loop(1, count, begin, 0)
    own.start()
    own.wait()

    def finish(s, c):
        other, _, send = copy(s)

        @pl.when(other < kept)
        def _():
            send.wait_send()

        @pl.when(me < kept)
        def _():
            send.wait_recv()

        return c

    lax.fori_loop(1, count, finish, 0)


def exchange(blocks, rows, cols, wide, cid):
    count = rows * cols if wide else cols
    kept = blocks.shape[0]
    return pl.pallas_call(
        functools.partial(exchange_kernel, rows, cols, wide, kept, cid),
        out_shape=jax.ShapeDtypeStruct((count,) + blocks.shape[1:], blocks.dtype),
        in_specs=[pl.BlockSpec(memory_space=pl.ANY)],
        out_specs=pl.BlockSpec(memory_space=pl.ANY),
        scratch_shapes=[
            pltpu.SemaphoreType.DMA((count,)),
            pltpu.SemaphoreType.DMA((count,)),
            pltpu.SemaphoreType.DMA,
        ],
        compiler_params=pltpu.CompilerParams(collective_id=cid, has_side_effects=True),
    )(blocks)


def roll_kernel(length, offs_ref, in_ref, out_ref):
    value = jnp.concatenate(
        [in_ref[s, 0].astype(f32) for s in range(in_ref.shape[0])], axis=1
    )
    offs = offs_ref[...]
    stride = 1
    while stride < length:
        chosen = (offs // stride) % 2 == 1
        value = jnp.where(chosen, pltpu.roll(value, length - stride, 1), value)
        stride *= 2
    out_ref[0] = value.astype(out_ref.dtype)


def remesh(blocks, offs):
    sources, groups, kb, yl = blocks.shape
    length = sources * yl
    return pl.pallas_call(
        functools.partial(roll_kernel, length),
        grid=(groups,),
        out_shape=jax.ShapeDtypeStruct((groups, kb, length), blocks.dtype),
        in_specs=[
            pl.BlockSpec((kb, 1), lambda i: (0, 0)),
            pl.BlockSpec((sources, 1, kb, yl), lambda i: (0, i, 0, 0)),
        ],
        out_specs=pl.BlockSpec((1, kb, length), lambda i: (i, 0, 0)),
    )(offs.reshape(kb, 1), blocks)


def dot(a, b):
    return jnp.dot(a, b, preferred_element_type=f32)


def greet_all(count, me, place):
    barrier = pltpu.get_barrier_semaphore()

    def greet(s, c):
        pl.semaphore_signal(
            barrier,
            inc=1,
            device_id=place((me + s) % count),
            device_id_type=pl.DeviceIdType.MESH,
        )
        return c

    lax.fori_loop(1, count, greet, 0)
    return lambda: pl.semaphore_wait(barrier, count - 1)


def back_kernel(
    rows, cols, nx, ny, nz, kept,
    in_ref, state_ref, strain_ref, inverse_ref, forward_ref, table_ref, out_ref,
    inverse, forward, table, products, away, modes, lines, block,
    inverse_sem, forward_sem, table_sem,
    far_send, far_recv, far_own, send_sem, recv_sem, own_sem,
):
    row, col = lax.axis_index("row"), lax.axis_index("col")
    count = rows * cols
    me = row * cols + col
    groups, kb, _ = state_ref.shape
    yl = ny // cols
    half = table_ref.shape[0] // 2
    gn = count // nz
    gb = in_ref.shape[1] // 3
    first_k = me * kb
    live = me < kept

    def place(d):
        return (d // cols, d % cols)

    wait_all = greet_all(count, me, place)

    def fetch(source, target, sem, i):
        return pltpu.make_async_copy(source.at[i], target.at[i], sem.at[i])

    triples = (
        (inverse_ref, inverse, inverse_sem),
        (forward_ref, forward, forward_sem),
        (table_ref, table, table_sem),
    )
    for triple in triples:
        for i in range(triple[0].shape[0]):
            fetch(*triple, i).start()

    piece = inverse_ref.shape[1]
    for i in range(inverse_ref.shape[0]):
        fetch(*triples[0], i).wait()
        velocity = dot(inverse[i], in_ref[...])
        v = [velocity[:, c * gb : (c + 1) * gb] for c in range(3)]
        for e, (one, two) in enumerate(pairs):
            products[i * piece : (i + 1) * piece, e * gb : (e + 1) * gb] = (
                v[one] * v[two]
            ).astype(bf16)
    for i in range(forward_ref.shape[0]):
        fetch(*triples[1], i).wait()
    wait_all()

    def far(s):
        other = (me + s) % count
        return pltpu.make_async_remote_copy(
            src_ref=away.at[jnp.minimum(other, kept - 1)],
            dst_ref=modes.at[me],
            send_sem=far_send.at[s],
            recv_sem=far_recv.at[s],
            device_id=place(other),
            device_id_type=pl.DeviceIdType.MESH,
        )

    tiles = forward_ref.shape[0]
    per = forward_ref.shape[1] // (2 * kb)

    def tile(step, c):
        t = (me // per + 1 + step) % tiles
        found = dot(forward[t], products[...]).astype(bf16)
        for h in range(per):
            away[t * per + h] = found[h * 2 * kb : (h + 1) * 2 * kb]
        for h in range(per):
            d = t * per + (me + h) % per

            @pl.when((d != me) & (d < kept))
            def _():
                far((d - me + count) % count).start()

        return c

    lax.fori_loop(0, tiles, tile, 0)
    far_copy = pltpu.make_async_copy(
        away.at[jnp.minimum(me, kept - 1)], modes.at[me], far_own
    )
    far_copy.start()
    for i in range(2 * half):
        fetch(*triples[2], i).wait()
    far_copy.wait()

    def send(z, s):
        other = (col + s) % cols
        return pltpu.make_async_remote_copy(
            src_ref=block.at[z, other],
            dst_ref=out_ref.at[col, z],
            send_sem=send_sem.at[z, s],
            recv_sem=recv_sem.at[z, s],
            device_id=(row, other),
            device_id_type=pl.DeviceIdType.MESH,
        )

    def make(z, j):
        used = live & ((j < half) | (j >= cols - half))
        columns = pl.ds(pl.multiple_of(j * yl, yl), yl)

        @pl.when(used)
        def _():
            i = jnp.where(j < half, j, j - (cols - 2 * half))
            both = dot(lines[...], table[i])
            kx = first_k + lax.broadcasted_iota(jnp.int32, (kb, yl), 0)
            ky = j * yl + lax.broadcasted_iota(jnp.int32, (kb, yl), 1)
            ys = jnp.where(ky < ny // 2, ky, ky - ny)
            k1 = (2.0 * math.pi / nx) * kx.astype(f32)
            k2 = (2.0 * math.pi / ny) * ys.astype(f32) - strain_ref[...] * k1
            retain = (3 * kx < nx) & (3 * jnp.abs(ys) < ny)
            found = []
            for e in range(n_pairs):
                a = both[2 * e * kb : (2 * e + 1) * kb]
                b = both[(2 * e + 1) * kb : (2 * e + 2) * kb]
                found.append((a[:, :yl] + b[:, yl:], b[:, :yl] - a[:, yl:]))
            for l in range(3):
                e0, e1 = pair_table[l]
                flux_real = k1 * found[e0][0] + k2 * found[e1][0]
                flux_imag = k1 * found[e0][1] + k2 * found[e1][1]
                for p, update in ((0, flux_imag), (1, -flux_real)):
                    state = state_ref[(l * 2 + p) * nz + z, :, columns].astype(f32)
                    change = jnp.where(retain, dt_step * update, 0.0)
                    block[z, j, l * 2 + p] = (state + change).astype(bf16)

        @pl.when(jnp.logical_not(used))
        def _():
            for g in range(groups // nz):
                block[z, j, g] = state_ref[g * nz + z, :, columns]

    def plane(turn, c):
        z = (row * nz // rows + turn) % nz

        @pl.when(live)
        def _():
            def arrive(b, c):
                s = (me + count - (z * gn + b)) % count

                @pl.when(s != 0)
                def _():
                    far(s).wait_recv()

                return c

            lax.fori_loop(0, gn, arrive, 0)
            for b in range(gn):
                for e in range(n_pairs):
                    lines[2 * e * kb : 2 * (e + 1) * kb, b * gb : (b + 1) * gb] = modes[
                        z * gn + b, :, e * gb : (e + 1) * gb
                    ]

        def step(s, c):
            make(z, (col + s) % cols)
            send(z, s).start()
            return c

        lax.fori_loop(1, cols, step, 0)
        make(z, col)
        own = pltpu.make_async_copy(block.at[z, col], out_ref.at[col, z], own_sem)
        own.start()
        own.wait()
        return c

    lax.fori_loop(0, nz, plane, 0)

    def finish(s, c):
        for z in range(nz):
            send(z, s).wait()
        return c

    lax.fori_loop(1, cols, finish, 0)

    def sent(s, c):
        @pl.when((me + s) % count < kept)
        def _():
            far(s).wait_send()

        return c

    lax.fori_loop(1, count, sent, 0)


def back(arrived, state, strain, rows, cols, nx, ny, nz):
    groups, kb, _ = state.shape
    yl = ny // cols
    count = rows * cols
    gb = arrived.shape[1] // 3
    half = -(-(-(-ny // 3)) // yl)
    cosine, sine = waves(np.arange(ny), np.arange(ny), ny)
    table = np.stack(
        [
            np.concatenate([m[:, j * yl : (j + 1) * yl] for m in (cosine, sine)], 1)
            for j in range(cols)
            if j < half or j >= cols - half
        ]
    )
    inverse = x_inverse_table(nx, kb).reshape(4, nx // 4, nx)
    kept = -(-(-(-nx // 3)) // kb)
    per = 4
    tiles = -(-kept // per)
    forward = x_forward_table(nx, kb, tiles * per).reshape(tiles, per * 2 * kb, nx)
    whole = pl.BlockSpec(memory_space=pltpu.VMEM)
    far = pl.BlockSpec(memory_space=pl.ANY)
    dma = pltpu.SemaphoreType.DMA
    vmem = lambda *shape: pltpu.VMEM(shape, bf16)
    return pl.pallas_call(
        functools.partial(back_kernel, rows, cols, nx, ny, nz, kept),
        out_shape=jax.ShapeDtypeStruct((cols, nz, groups // nz, kb, yl), bf16),
        in_specs=[whole, whole, whole, far, far, far],
        out_specs=far,
        scratch_shapes=[
            vmem(*inverse.shape),
            vmem(*forward.shape),
            vmem(*table.shape),
            vmem(nx, n_pairs * gb),
            vmem(tiles * per, 2 * kb, n_pairs * gb),
            vmem(count, 2 * kb, n_pairs * gb),
            vmem(n_pairs * 2 * kb, ny),
            vmem(nz, cols, groups // nz, kb, yl),
            dma((inverse.shape[0],)),
            dma((tiles,)),
            dma((table.shape[0],)),
            dma((count,)),
            dma((count,)),
            dma,
            dma((nz, cols)),
            dma((nz, cols)),
            dma,
        ],
        compiler_params=pltpu.CompilerParams(
            collective_id=7, has_side_effects=True, vmem_limit_bytes=54 * 2**20
        ),
    )(
        arrived,
        state,
        strain.reshape(1, 1),
        jnp.asarray(inverse),
        jnp.asarray(forward),
        jnp.asarray(narrow(table)),
    )


def ahead_kernel(
    rows, cols, ny, nz,
    in_ref, offs_ref, table_ref, lines_ref, state_ref,
    table, came, state, block,
    table_sem, send_sem, recv_sem, own_sem, far_send, far_recv, far_own,
):
    row, col = lax.axis_index("row"), lax.axis_index("col")
    count = rows * cols
    me = row * cols + col
    groups, kb, yl = in_ref.shape[1:]
    gb = lines_ref.shape[2] // 3
    gn = count // nz
    tiles, _, wide = table_ref.shape
    width = wide // 2
    per = width // gb

    def place(d):
        return (d // cols, d % cols)

    wait_all = greet_all(count, me, place)

    def fetch(i):
        return pltpu.make_async_copy(table_ref.at[i], table.at[i], table_sem.at[i])

    def near(s):
        other = (col + s) % cols
        return pltpu.make_async_remote_copy(
            src_ref=in_ref.at[other],
            dst_ref=came.at[col],
            send_sem=send_sem.at[s],
            recv_sem=recv_sem.at[s],
            device_id=(row, other),
            device_id_type=pl.DeviceIdType.MESH,
        )

    wait_all()
    for s in range(1, cols):
        near(s).start()
    own = pltpu.make_async_copy(in_ref.at[col], came.at[col], own_sem)
    own.start()
    for i in range(tiles):
        fetch(i).start()
    for i in range(tiles):
        fetch(i).wait()
    own.wait()
    for s in range(1, cols):
        near(s).wait()

    def gather(g, c):
        top = pl.multiple_of(g * kb, kb)
        for s in range(cols):
            state[pl.ds(top, kb), s * yl : (s + 1) * yl] = came[s, g]
        return c

    lax.fori_loop(0, groups, gather, 0)

    def far(s):
        other = (me + s) % count
        return pltpu.make_async_remote_copy(
            src_ref=block.at[other],
            dst_ref=lines_ref.at[me],
            send_sem=far_send.at[s],
            recv_sem=far_recv.at[s],
            device_id=place(other),
            device_id_type=pl.DeviceIdType.MESH,
        )

    offs = offs_ref[...]

    def tile(step, c):
        t = (me // nz + step) % tiles
        both = dot(state[...], table[t])
        gy = t * width + lax.broadcasted_iota(jnp.int32, (kb, width), 1)
        turn = (offs * gy) % ny
        turn = jnp.where(turn < ny // 2, turn, turn - ny)
        angle = (2.0 * math.pi / ny) * turn.astype(f32)
        cosine, sine = jnp.cos(angle), jnp.sin(angle)
        for c in range(3):
            for z in range(nz):
                a = both[((c * 2) * nz + z) * kb : ((c * 2) * nz + z + 1) * kb]
                b = both[((c * 2 + 1) * nz + z) * kb : ((c * 2 + 1) * nz + z + 1) * kb]
                real = a[:, :width] - b[:, width:]
                imag = a[:, width:] + b[:, :width]
                turned = (cosine * real + sine * imag, cosine * imag - sine * real)
                for h in range(per):
                    d = z * gn + t * per + h
                    for p in range(2):
                        block[d, p * kb : (p + 1) * kb, c * gb : (c + 1) * gb] = turned[p][
                            :, h * gb : (h + 1) * gb
                        ].astype(bf16)
        for z in range(nz):
            for h in range(per):
                d = z * gn + t * per + h

                @pl.when(d != me)
                def _():
                    far((d - me + count) % count).start()

        return 0

    lax.fori_loop(0, tiles, tile, 0)
    far_copy = pltpu.make_async_copy(block.at[me], lines_ref.at[me], far_own)
    far_copy.start()

    def shift(g, c):
        top = pl.multiple_of(g * kb, kb)
        value = state[pl.ds(top, kb), :].astype(f32)
        stride = 1
        while stride < ny:
            chosen = (offs // stride) % 2 == 1
            value = jnp.where(chosen, pltpu.roll(value, ny - stride, 1), value)
            stride *= 2
        state_ref[g] = value.astype(bf16)
        return c

    lax.fori_loop(0, groups, shift, 0)
    far_copy.wait()

    def finish(s, c):
        far(s).wait()
        return c

    lax.fori_loop(1, count, finish, 0)


def ahead(parts, offs, rows, cols, ny, nz, gb):
    groups, kb, yl = parts.shape[1:]
    width = 2 * gb
    cosine, sine = waves(np.arange(ny), np.arange(ny), ny)
    table = np.stack(
        [
            np.concatenate([m[:, t : t + width] for m in (cosine, sine)], 1)
            for t in range(0, ny, width)
        ]
    )
    count = rows * cols
    whole = pl.BlockSpec(memory_space=pltpu.VMEM)
    far = pl.BlockSpec(memory_space=pl.ANY)
    dma = pltpu.SemaphoreType.DMA
    return pl.pallas_call(
        functools.partial(ahead_kernel, rows, cols, ny, nz),
        out_shape=(
            jax.ShapeDtypeStruct((count, 2 * kb, 3 * gb), bf16),
            jax.ShapeDtypeStruct((groups, kb, ny), bf16),
        ),
        in_specs=[far, whole, far],
        out_specs=(far, whole),
        scratch_shapes=[
            pltpu.VMEM(table.shape, bf16),
            pltpu.VMEM((cols, groups, kb, yl), bf16),
            pltpu.VMEM((groups * kb, ny), bf16),
            pltpu.VMEM((count, 2 * kb, 3 * gb), bf16),
            dma((table.shape[0],)),
            dma((cols,)),
            dma((cols,)),
            dma,
            dma((count,)),
            dma((count,)),
            dma,
        ],
        compiler_params=pltpu.CompilerParams(
            collective_id=6, has_side_effects=True, vmem_limit_bytes=44 * 2**20
        ),
    )(parts, offs.reshape(kb, 1), jnp.asarray(narrow(table)))


def local(velocity_modes, offsets, shear_steps):
    nz, yl, kl = velocity_modes.shape[2:]
    rows, cols = lax.axis_size("row"), lax.axis_size("col")
    devices = rows * cols
    ny, nk = yl * cols, kl * rows
    nx = 2 * nk
    kb = kl // cols
    gb = ny * nz // devices
    gn = ny // gb
    row, col = lax.axis_index("row"), lax.axis_index("col")
    strain = shear_steps[0].astype(f32) / period - 0.5

    parts = velocity_modes.reshape(6 * nz, yl, cols, kb).transpose(2, 0, 3, 1)
    offs = lax.dynamic_slice(offsets, (col * kb,), (kb,))
    aligned = kb % 16 == 0 and gb % 128 == 0 and yl % 128 == 0
    if aligned:
        lines, remeshed = ahead(parts, offs, rows, cols, ny, nz, gb)
    else:
        parts = exchange(parts, rows, cols, False, 1)
        remeshed = remesh(parts, offs)

        every = np.arange(ny)
        both = dot(remeshed.reshape(-1, ny), jnp.asarray(y_table(ny, every)))
        both = both.reshape(3, 2, nz, kb, 2, ny)
        real = both[:, 0, :, :, 0] - both[:, 1, :, :, 1]
        imag = both[:, 0, :, :, 1] + both[:, 1, :, :, 0]
        lines = jnp.stack([real, imag]).astype(bf16).reshape(2, 3, nz, kb, gn, gb)
        lines = lines.transpose(2, 4, 0, 3, 1, 5).reshape(devices, 2 * kb, 3 * gb)
        lines = exchange(lines, rows, cols, True, 2)
    lines = lines.reshape(2 * nk, 3 * gb)

    if aligned:
        parts = back(lines, remeshed, strain, rows, cols, nx, ny, nz)
        parts = parts.transpose(2, 1, 4, 0, 3)
        return parts.reshape(3, 2, nz, yl, kl)
    else:
        velocity = dot(jnp.asarray(x_inverse_table(nx, kb)), lines)
        v = [velocity[:, c * gb : (c + 1) * gb] for c in range(3)]
        products = jnp.concatenate([(v[a] * v[b]).astype(bf16) for a, b in pairs], 1)
        kept = -(-(-(-nx // 3)) // kb)
        x_modes = dot(jnp.asarray(x_forward_table(nx, kb, kept)), products).astype(bf16)
        x_modes = x_modes.reshape(kept, 2 * kb, n_pairs * gb)
        x_modes = exchange(x_modes, rows, cols, True, 3)

        x_modes = x_modes.reshape(nz, gn, 2, kb, n_pairs, gb).transpose(4, 2, 0, 3, 1, 5)
        low = -(-(-(-ny // 3)) // 128) * 128
        near = np.concatenate([np.arange(low), np.arange(ny - low, ny)])
        both = dot(x_modes.reshape(-1, ny), jnp.asarray(y_table(ny, near)))
        both = both.reshape(n_pairs, 2, nz, kb, 2, 2 * low)
        real = both[:, 0, :, :, 0] + both[:, 1, :, :, 1]
        imag = both[:, 1, :, :, 0] - both[:, 0, :, :, 1]

        kx = ((row * cols + col) * kb + jnp.arange(kb, dtype=jnp.int32))[:, None]
        ys = jnp.concatenate(
            [jnp.arange(low, dtype=jnp.int32), jnp.arange(-low, 0, dtype=jnp.int32)]
        )[None, :]
        k1 = 2.0 * math.pi * kx.astype(f32) / nx
        k2 = 2.0 * math.pi * ys.astype(f32) / ny - strain * k1
        retain = (3 * kx < nx) & (3 * jnp.abs(ys) < ny)
        update = []
        for l in range(3):
            e0, e1 = pair_table[l]
            flux_real = k1 * real[e0] + k2 * real[e1]
            flux_imag = k1 * imag[e0] + k2 * imag[e1]
            update.append(jnp.stack([flux_imag, -flux_real]))
        update = jnp.where(retain, dt_step * jnp.stack(update), 0.0)
        state = remeshed.reshape(3, 2, nz, kb, ny)
        advanced = jnp.concatenate(
            [
                (state[..., :low].astype(f32) + update[..., :low]).astype(bf16),
                state[..., low : ny - low],
                (state[..., ny - low :].astype(f32) + update[..., low:]).astype(bf16),
            ],
            -1,
        )
        parts = advanced.reshape(6 * nz, kb, cols, yl).transpose(2, 0, 1, 3)
        parts = exchange(parts, rows, cols, False, 4)
    out = parts.transpose(1, 3, 0, 2)
    return out.reshape(3, 2, nz, yl, kl)


def solution(mesh):
    return jax.shard_map(
        local,
        mesh=mesh,
        in_specs=(P(None, None, None, "col", "row"), P("row"), P()),
        out_specs=P(None, None, None, "col", "row"),
        check_vma=False,
    )
```
